32 devices in a mesh: ctx: 4 (over z), row: 2 (over y), col: 4 (over x, core).
Axes of the slice: x: 2, y: 2, z: 4, core: 2. Of those that a mesh axis runs over, the one named last changes fastest.
Arguments:
- tokens: bfloat16 [2048, 8192], P(('ctx', 'row'), 'col'), may hold values from -9 to 9
- w_query: bfloat16 [8192, 2048], P('ctx', 'col'), may hold values from -0.0625 to 0.0625
- key_value_weight: bfloat16 [8192, 512], P('ctx', 'col'), may hold values from -0.0625 to 0.0625
- segment: int32 [2048], P(('ctx', 'row')), may hold values from 0 to 7, never falling along the last dimension, each value on 1 to 1024 neighbouring positions
Outputs:
- attended: bfloat16 [2048, 2048], P(('ctx', 'row'), 'col')
The draws below stay inside these ranges and needn't reach their ends.
Inputs may be any that keep to these rules, and one draw needn't show every extreme that they name: `segment`: document ids never fall along the sequence; a document holds 1 to 1024 tokens.
All inputs are finite; a program needn't handle non-finite values.
Results may differ from the reference program's by a relative error of at most 0.011.
Values may be sent and summed in bfloat16 or wider, within the bound.
A program may use at most 64 MiB of HBM per device.

```python
import math
import jax
import jax.numpy as jnp
import numpy as np
from jax import lax

MODEL_WIDTH = 8192
HEAD_WIDTH = 128
BLOCK_TOKENS = 512
QUERY_HEADS = 16
KEY_VALUE_HEADS = 2
SEQUENCE_TOKENS = 2048
N_CTX = 4


def draw_tokens(key, part):
    first = jax.random.fold_in(key, 0)
    values = jnp.clip(jax.random.normal(first, (SEQUENCE_TOKENS, MODEL_WIDTH), jnp.float32), -4.0, 4.0)
    return values.astype(jnp.bfloat16)


def block_scale(stream_key, shape, pieces, smallest, high):
    gain, own = 1.0, jax.random.fold_in(stream_key, 6)
    for dim, blocks in pieces:
        steps = jnp.exp(jax.random.uniform(jax.random.fold_in(own, dim), (blocks,), jnp.float32, smallest / len(pieces), high / len(pieces)))
        gain = gain * jnp.repeat(steps, shape[dim] // blocks).reshape([-1 if axis == dim else 1 for axis in range(len(shape))])
    return gain


def profile(number_of, total, bound, lean):
    loads = [(1 << 20) // math.isqrt(standing ** lean) + 1 for standing in range(2, number_of + 1)]
    spare, given = total - bound - (number_of - 1), [1] * (number_of - 1)
    while spare > 0:
        free = [i for i in range(number_of - 1) if given[i] < bound]
        whole, remaining = sum([loads[i] for i in free]), spare
        for i in free:
            extra = min(bound - given[i], max(1, remaining * loads[i] // whole), spare)
            given[i] = given[i] + extra
            spare = spare - extra
    return np.array([bound] + given)


def uneven(own_key, count, total, most, lean):
    if count == 2:
        one = jax.random.randint(own_key, (), max(1, total - most), min(most, total - 1) + 1)
        return jnp.stack([one, total - one])
    sizes = jnp.asarray(profile(count, total, most, lean), jnp.int32)
    twos = (count - 1) // 2
    giver, receiver = sizes[1:1 + 2 * twos:2], sizes[2:2 + 2 * twos:2]
    margin = jnp.minimum(giver - 1, most - receiver)
    passed = jax.random.randint(jax.random.fold_in(own_key, 1), (twos,), 0, 1 << 20) % (margin + 1)
    sizes = sizes.at[1:1 + 2 * twos:2].set(giver - passed).at[2:2 + 2 * twos:2].set(receiver + passed)
    return sizes[jax.random.permutation(jax.random.fold_in(own_key, 2), count)]


def normal_values(own_key, dims, deviation, limit, cuts=(), kind=jnp.bfloat16):
    gain = block_scale(own_key, dims, cuts, -0.22, 0.18) if cuts else 1.0
    drawn = jax.random.normal(own_key, dims, jnp.float32) * deviation * gain
    return jnp.minimum(jnp.maximum(drawn, -limit), limit).astype(kind)


def setup_inputs(seed: int = 0) -> dict:
    arg_keys = jax.random.split(jax.random.key(seed), 5)
    return {
        "tokens": draw_tokens(jax.random.fold_in(arg_keys[4], 71), 0),
        "w_query": normal_values(arg_keys[1], (MODEL_WIDTH, QUERY_HEADS * HEAD_WIDTH), MODEL_WIDTH ** -0.5, 0.0625, ((0, 4), (1, 4))),
        "key_value_weight": normal_values(arg_keys[2], (MODEL_WIDTH, 2 * KEY_VALUE_HEADS * HEAD_WIDTH), MODEL_WIDTH ** -0.5, 0.0625, ((0, 4), (1, 4))),
        "segment": jnp.searchsorted(jnp.cumsum(uneven(arg_keys[3], 2 * N_CTX, SEQUENCE_TOKENS, 2 * BLOCK_TOKENS, 1)), jnp.arange(SEQUENCE_TOKENS), side="right").astype(jnp.int32),
    }


def reference(tokens, w_query, key_value_weight, segment):
    query = jnp.dot(tokens, w_query, preferred_element_type=jnp.float32).astype(jnp.bfloat16)
    key_value_rows = jnp.dot(tokens, key_value_weight, preferred_element_type=jnp.float32).astype(jnp.bfloat16)
    query = query.reshape(SEQUENCE_TOKENS // BLOCK_TOKENS, BLOCK_TOKENS, QUERY_HEADS, HEAD_WIDTH)
    key_value_rows = key_value_rows.reshape(SEQUENCE_TOKENS, KEY_VALUE_HEADS, 2, HEAD_WIDTH)
    padded_tokens = jnp.concatenate([jnp.zeros((BLOCK_TOKENS, KEY_VALUE_HEADS, 2, HEAD_WIDTH), jnp.bfloat16), key_value_rows], axis=0)
    seg_padded = jnp.concatenate([jnp.full((BLOCK_TOKENS,), -1, jnp.int32), segment.astype(jnp.int32)], axis=0)
    scale = 1.0 / math.sqrt(HEAD_WIDTH)
    query_group = QUERY_HEADS // KEY_VALUE_HEADS

    def one_block(index):
        start = (index * BLOCK_TOKENS).astype(jnp.int32)
        queries = query[index].astype(jnp.float32)
        window = lax.dynamic_slice_in_dim(padded_tokens, start, 2 * BLOCK_TOKENS, 0)
        key_seg = lax.dynamic_slice_in_dim(seg_padded, start, 2 * BLOCK_TOKENS, 0)
        query_seg = lax.dynamic_slice_in_dim(segment.astype(jnp.int32), start, BLOCK_TOKENS, 0)
        keys = jnp.repeat(window[:, :, 0], query_group, axis=1).astype(jnp.float32)
        values = jnp.repeat(window[:, :, 1], query_group, axis=1).astype(jnp.float32)
        query_pos = jnp.arange(BLOCK_TOKENS) + BLOCK_TOKENS
        key_pos = jnp.arange(2 * BLOCK_TOKENS)
        allow = (key_pos[None, :] <= query_pos[:, None]) & (query_seg[:, None] == key_seg[None, :])
        score = jnp.einsum('qhd,khd->hqk', queries, keys) * scale
        score = jnp.where(allow[None], score, -jnp.inf)
        top = lax.optimization_barrier(jnp.max(score, axis=-1, keepdims=True))
        weight = jnp.exp(score - top)
        total = lax.optimization_barrier(jnp.sum(weight, axis=-1))
        probs = weight.astype(jnp.bfloat16).astype(jnp.float32)
        numer = jnp.einsum('hqk,khd->qhd', probs, values)
        out = numer / jnp.transpose(total)[:, :, None]
        return out.astype(jnp.bfloat16).reshape(BLOCK_TOKENS, QUERY_HEADS * HEAD_WIDTH)
    result = lax.map(one_block, jnp.arange(SEQUENCE_TOKENS // BLOCK_TOKENS, dtype=jnp.int32))
    return result.reshape(SEQUENCE_TOKENS, QUERY_HEADS * HEAD_WIDTH)
```

```python
import functools
import math

import jax
import jax.numpy as jnp
from jax import lax
from jax.experimental import pallas as pl
from jax.experimental.pallas import tpu as pltpu
from jax.sharding import PartitionSpec as P

MESH = pl.DeviceIdType.MESH


def kernel(
    n, head, tok_hbm, wq_hbm, wkv_hbm, seg_ref, out_ref,
    whole, weights, part, landed, own, query, window, segs,
    w_sem, a2a_send, tok_recv, fwd_send, part_send, part_recv, kv_send, kv_recv, seg_send, seg_recv,
):
    c, r, k = lax.axis_index("ctx"), lax.axis_index("row"), lax.axis_index("col")
    half = tok_hbm.shape[0]
    rows = half // n
    width = weights.shape[1]
    even = k % 2 == 0

    w_copies = [
        pltpu.make_async_copy(wkv_hbm, weights.at[:, pl.ds(0, head)], w_sem.at[0]),
        pltpu.make_async_copy(wq_hbm, weights.at[:, pl.ds(head, width - head)], w_sem.at[1]),
    ]
    for copy in w_copies:
        copy.start()

    barrier = pltpu.get_barrier_semaphore()

    def greet(i, carry):
        c2, k2 = i // n, i % n

        @pl.when(i != c * n + k)
        def _():
            pl.semaphore_signal(barrier, inc=1, device_id=(c2, r, k2), device_id_type=MESH)

        return carry

    lax.fori_loop(0, n * n, greet, 0)
    for dc in (-1, 0, 1):

        @pl.when((c + dc >= 0) & (c + dc < n))
        def _():
            for dk in (0, 1):
                pl.semaphore_signal(barrier, inc=1, device_id=(c + dc, 1 - r, k ^ dk), device_id_type=MESH)

    ends = jnp.where(c == 0, 1, 0) + jnp.where(c == n - 1, 1, 0)
    pl.semaphore_wait(barrier, n * n - 1 + 6 - 2 * ends)

    def piece(block, j):
        return whole.at[block, pl.ds(pl.multiple_of(j * rows, rows), rows)]

    def landing(ref, sem):
        return pltpu.make_async_copy(ref, ref, sem)

    order = [m for m in range(n) if m & 2] + [m for m in range(n) if not m & 2]

    def scatter(m):
        j = k ^ m
        return pltpu.make_async_remote_copy(
            src_ref=tok_hbm.at[pl.ds(pl.multiple_of(j * rows, rows), rows)],
            dst_ref=piece(c, j),
            send_sem=a2a_send.at[m],
            recv_sem=tok_recv.at[c, j],
            device_id=(k, r, j),
            device_id_type=MESH,
        )

    for m in order:
        if m == 0:

            @pl.when(c == k)
            def _():
                pltpu.make_async_copy(
                    tok_hbm.at[pl.ds(pl.multiple_of(k * rows, rows), rows)], piece(c, k), tok_recv.at[c, k]
                ).start()

            @pl.when(c != k)
            def _():
                scatter(0).start()

        else:
            scatter(m).start()

    seg_slot = 2 + r

    def seg_copy(i):
        dc, r2 = ((0, 1 - r), (1, r), (1, 1 - r))[i]
        slot = 2 + r if dc == 0 else r
        return pltpu.make_async_remote_copy(
            src_ref=seg_ref, dst_ref=segs.at[slot], send_sem=seg_send.at[i], recv_sem=seg_recv.at[slot],
            device_id=(c + dc, r2, k), device_id_type=MESH,
        )

    seg_copy(0).start()

    @pl.when(c < n - 1)
    def _():
        seg_copy(1).start()
        seg_copy(2).start()

    segs[seg_slot] = seg_ref[...]

    def forward(s, block, j, to, index):
        return pltpu.make_async_remote_copy(
            src_ref=piece(block, j), dst_ref=piece(block, j),
            send_sem=fwd_send.at[s, index], recv_sem=tok_recv.at[block, j],
            device_id=(c, r, to), device_id_type=MESH,
        )

    peers = list(range(2, n, 2))

    def step_a(s):
        block = c ^ s
        landing(piece(block, k), tok_recv.at[block, k]).wait()
        for i, m in enumerate(peers):
            forward(s, block, k, k ^ m, i).start()
        forward(s, block, k, k ^ 1, len(peers)).start()

    def step_b(s):
        block = c ^ s
        for i, m in enumerate(peers):
            landing(piece(block, k ^ m), tok_recv.at[block, k ^ m]).wait()
            forward(s, block, k ^ m, k ^ 1, len(peers) + 1 + i).start()

    def part_copy(s):
        return pltpu.make_async_remote_copy(
            src_ref=part.at[s - 1], dst_ref=landed.at[s - 1],
            send_sem=part_send.at[s - 1], recv_sem=part_recv.at[s - 1],
            device_id=(c ^ s, r, k), device_id_type=MESH,
        )

    spans = [(0, head)] + [(lo, min(256, width - lo)) for lo in range(head, width, 256)]

    def step_c(s):
        block = c ^ s
        for m in [0] + peers:
            landing(piece(block, k ^ 1 ^ m), tok_recv.at[block, k ^ 1 ^ m]).wait()
        if s == 0:
            for copy in w_copies:
                copy.wait()
        for lo, size in spans:
            product = jnp.dot(whole[block], weights[:, lo : lo + size], preferred_element_type=jnp.float32)
            if s == 0:
                own[:, lo : lo + size] = product
            else:
                part[s - 1, :, lo : lo + size] = product.astype(jnp.bfloat16)
        if s:
            part_copy(s).start()

    for t in range(n + 2):
        if t < n:
            step_a(t)
        if 0 <= t - 1 < n:
            step_b(t - 1)
        if 0 <= t - 2 < n:
            step_c(t - 2)

    for s in range(1, n):
        landing(landed.at[s - 1], part_recv.at[s - 1]).wait()

    def summed(lo, size):
        total = own[:, lo : lo + size]
        for s in range(1, n):
            total = total + landed[s - 1, :, lo : lo + size].astype(jnp.float32)
        return total.astype(jnp.bfloat16)

    kind = k % 2
    window[kind, 2 + r] = summed(0, head)

    def kv_copy(i):
        dc, dr, dk = i // 4, (i // 2) % 2, i % 2
        r2 = 1 - r if dr else r
        slot = 2 + r if dc == 0 else r
        return pltpu.make_async_remote_copy(
            src_ref=window.at[kind, 2 + r], dst_ref=window.at[kind, slot],
            send_sem=kv_send.at[i], recv_sem=kv_recv.at[kind, slot],
            device_id=(c + dc, r2, k ^ dk), device_id_type=MESH,
        )

    @pl.when(c < n - 1)
    def _():
        for i in (6, 7, 4, 5):
            kv_copy(i).start()

    for i in (2, 3, 1):
        kv_copy(i).start()

    @pl.when(c == 0)
    def _():
        for slot in (0, 1):
            for which in (0, 1):
                window[which, slot] = jnp.zeros((half, head), jnp.bfloat16)
            segs[slot] = jnp.zeros(segs.shape[1:], jnp.int32)

    query[...] = summed(head, width - head)

    landing(segs.at[3 - r], seg_recv.at[3 - r]).wait()

    @pl.when(c > 0)
    def _():
        for slot in (0, 1):
            landing(segs.at[slot], seg_recv.at[slot]).wait()

    key_seg = jnp.concatenate([segs[i][:1] for i in range(4)], axis=1)
    mine = jnp.transpose(jnp.broadcast_to(seg_ref[:1], (128, half)))[:, :1]
    keys_n = 4 * half
    key_pos = lax.broadcasted_iota(jnp.int32, (half, keys_n), 1)
    query_pos = lax.broadcasted_iota(jnp.int32, (half, keys_n), 0) + (2 + r) * half
    first = jnp.where(c == 0, 2 * half, 0)
    allow = (key_pos <= query_pos) & (mine == key_seg) & (key_pos >= first)

    landing(window.at[1 - kind, 2 + r], kv_recv.at[1 - kind, 2 + r]).wait()
    for which in (0, 1):
        landing(window.at[which, 3 - r], kv_recv.at[which, 3 - r]).wait()

    @pl.when(c > 0)
    def _():
        for which in (0, 1):
            for slot in (0, 1):
                landing(window.at[which, slot], kv_recv.at[which, slot]).wait()

    keys = window[0].reshape(keys_n, head)
    values = window[1].reshape(keys_n, head)
    scale = 1.0 / math.sqrt(head)
    for h in range((width - head) // head):
        score = lax.dot_general(
            query[:, h * head : (h + 1) * head], keys, (((1,), (1,)), ((), ())), preferred_element_type=jnp.float32
        )
        score = jnp.where(allow, score * scale, -jnp.inf)
        weight = jnp.exp(score - jnp.max(score, axis=1, keepdims=True))
        total = jnp.sum(weight, axis=1, keepdims=True)
        numer = jnp.dot(weight.astype(jnp.bfloat16), values, preferred_element_type=jnp.float32)
        out_ref[:, h * head : (h + 1) * head] = (numer / total).astype(jnp.bfloat16)

    for m in range(1, n):
        scatter(m).wait_send()

    @pl.when(c != k)
    def _():
        scatter(0).wait_send()

    for s in range(n):
        block = c ^ s
        for i in range(2 * len(peers) + 1):
            forward(s, block, k, k ^ 1, i).wait_send()
    for s in range(1, n):
        part_copy(s).wait_send()
    for i in (1, 2, 3):
        kv_copy(i).wait_send()
    seg_copy(0).wait_send()

    @pl.when(c < n - 1)
    def _():
        for i in (4, 5, 6, 7):
            kv_copy(i).wait_send()
        seg_copy(1).wait_send()
        seg_copy(2).wait_send()


def local(n, tokens, w_query, key_value_weight, segment):
    half, depth = tokens.shape
    head = key_value_weight.shape[1]
    width = head + w_query.shape[1]
    seg = jnp.broadcast_to(segment[None, :], (8, half))
    hbm = pl.BlockSpec(memory_space=pl.ANY)
    vmem = pl.BlockSpec(memory_space=pltpu.VMEM)
    dma = pltpu.SemaphoreType.DMA
    return pl.pallas_call(
        functools.partial(kernel, n, head),
        out_shape=jax.ShapeDtypeStruct((half, w_query.shape[1]), jnp.bfloat16),
        in_specs=[hbm, hbm, hbm, vmem],
        out_specs=vmem,
        scratch_shapes=[
            pltpu.VMEM((n, half, depth), jnp.bfloat16),
            pltpu.VMEM((depth, width), jnp.bfloat16),
            pltpu.VMEM((n - 1, half, width), jnp.bfloat16),
            pltpu.VMEM((n - 1, half, width), jnp.bfloat16),
            pltpu.VMEM((half, width), jnp.float32),
            pltpu.VMEM((half, width - head), jnp.bfloat16),
            pltpu.VMEM((2, 4, half, head), jnp.bfloat16),
            pltpu.VMEM((4, 8, half), jnp.int32),
            dma((2,)),
            dma((n,)),
            dma((n, n)),
            dma((n, n)),
            dma((n - 1,)),
            dma((n - 1,)),
            dma((8,)),
            dma((2, 4)),
            dma((3,)),
            dma((4,)),
        ],
        compiler_params=pltpu.CompilerParams(
            collective_id=0, has_side_effects=True, vmem_limit_bytes=50 * 2**20
        ),
    )(tokens, w_query, key_value_weight, seg)


def solution(mesh):
    in_specs = (P(("ctx", "row"), "col"), P("ctx", "col"), P("ctx", "col"), P(("ctx", "row")))
    out_specs = P(("ctx", "row"), "col")
    step = functools.partial(local, mesh.shape["ctx"])
    return jax.shard_map(step, mesh=mesh, in_specs=in_specs, out_specs=out_specs, check_vma=False)
```

```python
import functools
import math

import jax
import jax.numpy as jnp
from jax import lax
from jax.experimental import pallas as pl
from jax.experimental.pallas import tpu as pltpu
from jax.sharding import PartitionSpec as P

MESH = pl.DeviceIdType.MESH


def kernel(
    n, head, tok_hbm, wq_hbm, wkv_hbm, seg_ref, out_ref,
    whole, staged, weights, part, landed, own, query, window, segs,
    w_sem, a2a_send, stage_recv, relay_send, tok_recv, fwd_send, part_send, part_recv, kv_send, kv_recv, seg_send, seg_recv,
):
    c, r, k = lax.axis_index("ctx"), lax.axis_index("row"), lax.axis_index("col")
    half = tok_hbm.shape[0]
    rows = half // n
    width = weights.shape[1]
    even = k % 2 == 0

    w_copies = [
        pltpu.make_async_copy(wkv_hbm, weights.at[:, pl.ds(0, head)], w_sem.at[0]),
        pltpu.make_async_copy(wq_hbm, weights.at[:, pl.ds(head, width - head)], w_sem.at[1]),
    ]
    for copy in w_copies:
        copy.start()

    barrier = pltpu.get_barrier_semaphore()

    def greet(i, carry):
        c2, k2 = i // n, i % n

        @pl.when(i != c * n + k)
        def _():
            pl.semaphore_signal(barrier, inc=1, device_id=(c2, r, k2), device_id_type=MESH)

        return carry

    lax.fori_loop(0, n * n, greet, 0)
    for dc in (-1, 0, 1):

        @pl.when((c + dc >= 0) & (c + dc < n))
        def _():
            for dk in (0, 1):
                pl.semaphore_signal(barrier, inc=1, device_id=(c + dc, 1 - r, k ^ dk), device_id_type=MESH)

    ends = jnp.where(c == 0, 1, 0) + jnp.where(c == n - 1, 1, 0)
    pl.semaphore_wait(barrier, n * n - 1 + 6 - 2 * ends)

    def piece(block, j):
        return whole.at[block, pl.ds(pl.multiple_of(j * rows, rows), rows)]

    def landing(ref, sem):
        return pltpu.make_async_copy(ref, ref, sem)

    own_plane = c == k

    def token_rows(j):
        return tok_hbm.at[pl.ds(pl.multiple_of(j * rows, rows), rows)]

    def scatter(m, plane):
        j = k ^ m
        return pltpu.make_async_remote_copy(
            src_ref=token_rows(j), dst_ref=piece(c, j), send_sem=a2a_send.at[m], recv_sem=tok_recv.at[c, j],
            device_id=(plane, r, j), device_id_type=MESH,
        )

    def stage(m):
        j = k ^ m
        return pltpu.make_async_remote_copy(
            src_ref=token_rows(j), dst_ref=staged.at[m], send_sem=a2a_send.at[m], recv_sem=stage_recv.at[m],
            device_id=(c, r, j), device_id_type=MESH,
        )

    def relay(m):
        return pltpu.make_async_remote_copy(
            src_ref=staged.at[m], dst_ref=piece(c, k), send_sem=relay_send.at[m], recv_sem=tok_recv.at[c, k],
            device_id=(k ^ m, r, k), device_id_type=MESH,
        )

    far = list(range(2, n))

    @pl.when(own_plane)
    def _():
        for m in far:
            scatter(m, c).start()
        pltpu.make_async_copy(token_rows(k), piece(c, k), tok_recv.at[c, k]).start()
        scatter(1, c).start()

    @pl.when(c != k)
    def _():
        for m in far:
            stage(m).start()
        for m in (1, 0):
            scatter(m, k).start()

    segs[2 + r] = jnp.broadcast_to(seg_ref[...], segs.shape[1:])

    def seg_copy(i):
        dc, r2 = ((0, 1 - r), (1, r), (1, 1 - r))[i]
        slot = 2 + r if dc == 0 else r
        return pltpu.make_async_remote_copy(
            src_ref=segs.at[2 + r], dst_ref=segs.at[slot], send_sem=seg_send.at[i], recv_sem=seg_recv.at[slot],
            device_id=(c + dc, r2, k), device_id_type=MESH,
        )

    seg_copy(0).start()

    @pl.when(c < n - 1)
    def _():
        seg_copy(1).start()
        seg_copy(2).start()

    for m in far:

        @pl.when(c != k ^ m)
        def _():
            landing(staged.at[m], stage_recv.at[m]).wait()
            relay(m).start()

    def forward(s, block, j, to, index):
        return pltpu.make_async_remote_copy(
            src_ref=piece(block, j), dst_ref=piece(block, j),
            send_sem=fwd_send.at[s, index], recv_sem=tok_recv.at[block, j],
            device_id=(c, r, to), device_id_type=MESH,
        )

    peers = list(range(2, n, 2))

    def step_a(s):
        block = c ^ s
        landing(piece(block, k), tok_recv.at[block, k]).wait()
        for i, m in enumerate(peers):
            forward(s, block, k, k ^ m, i).start()
        forward(s, block, k, k ^ 1, len(peers)).start()

    def step_b(s):
        block = c ^ s
        for i, m in enumerate(peers):
            landing(piece(block, k ^ m), tok_recv.at[block, k ^ m]).wait()
            forward(s, block, k ^ m, k ^ 1, len(peers) + 1 + i).start()

    def part_copy(s):
        return pltpu.make_async_remote_copy(
            src_ref=part.at[s - 1], dst_ref=landed.at[s - 1],
            send_sem=part_send.at[s - 1], recv_sem=part_recv.at[s - 1],
            device_id=(c ^ s, r, k), device_id_type=MESH,
        )

    spans = [(0, head)] + [(lo, min(256, width - lo)) for lo in range(head, width, 256)]

    def step_c(s):
        block = c ^ s
        for m in [0] + peers:
            landing(piece(block, k ^ 1 ^ m), tok_recv.at[block, k ^ 1 ^ m]).wait()
        if s == 0:
            for copy in w_copies:
                copy.wait()
        for lo, size in spans:
            product = jnp.dot(whole[block], weights[:, lo : lo + size], preferred_element_type=jnp.float32)
            if s == 0:
                own[:, lo : lo + size] = product
            else:
                part[s - 1, :, lo : lo + size] = product.astype(jnp.bfloat16)
        if s:
            part_copy(s).start()

    for t in range(n + 2):
        if t < n:
            step_a(t)
        if 0 <= t - 1 < n:
            step_b(t - 1)
        if 0 <= t - 2 < n:
            step_c(t - 2)

    for s in range(1, n):
        landing(landed.at[s - 1], part_recv.at[s - 1]).wait()

    def summed(lo, size):
        total = own[:, lo : lo + size]
        for s in range(1, n):
            total = total + landed[s - 1, :, lo : lo + size].astype(jnp.float32)
        return total.astype(jnp.bfloat16)

    kind = k % 2
    window[kind, 2 + r] = summed(0, head)

    def kv_copy(i):
        dc, dr, dk = i // 4, (i // 2) % 2, i % 2
        r2 = 1 - r if dr else r
        slot = 2 + r if dc == 0 else r
        return pltpu.make_async_remote_copy(
            src_ref=window.at[kind, 2 + r], dst_ref=window.at[kind, slot],
            send_sem=kv_send.at[i], recv_sem=kv_recv.at[kind, slot],
            device_id=(c + dc, r2, k ^ dk), device_id_type=MESH,
        )

    @pl.when(c < n - 1)
    def _():
        for i in (6, 7, 4, 5):
            kv_copy(i).start()

    for i in (2, 3, 1):
        kv_copy(i).start()

    @pl.when(c == 0)
    def _():
        for slot in (0, 1):
            for which in (0, 1):
                window[which, slot] = jnp.zeros((half, head), jnp.bfloat16)
            segs[slot] = jnp.zeros(segs.shape[1:], jnp.int32)

    query[...] = summed(head, width - head)

    landing(segs.at[3 - r], seg_recv.at[3 - r]).wait()

    @pl.when(c > 0)
    def _():
        for slot in (0, 1):
            landing(segs.at[slot], seg_recv.at[slot]).wait()

    key_seg = jnp.concatenate([segs[i][:1] for i in range(4)], axis=1)
    mine = jnp.transpose(jnp.broadcast_to(seg_ref[...], (128, half)))[:, :1]
    keys_n = 4 * half
    key_pos = lax.broadcasted_iota(jnp.int32, (half, keys_n), 1)
    query_pos = lax.broadcasted_iota(jnp.int32, (half, keys_n), 0) + (2 + r) * half
    first = jnp.where(c == 0, 2 * half, 0)
    allow = (key_pos <= query_pos) & (mine == key_seg) & (key_pos >= first)

    landing(window.at[1 - kind, 2 + r], kv_recv.at[1 - kind, 2 + r]).wait()
    for which in (0, 1):
        landing(window.at[which, 3 - r], kv_recv.at[which, 3 - r]).wait()

    @pl.when(c > 0)
    def _():
        for which in (0, 1):
            for slot in (0, 1):
                landing(window.at[which, slot], kv_recv.at[which, slot]).wait()

    keys = window[0].reshape(keys_n, head)
    values = window[1].reshape(keys_n, head)
    scale = 1.0 / math.sqrt(head)
    for h in range((width - head) // head):
        score = lax.dot_general(
            query[:, h * head : (h + 1) * head], keys, (((1,), (1,)), ((), ())), preferred_element_type=jnp.float32
        )
        score = jnp.where(allow, score * scale, -jnp.inf)
        weight = jnp.exp(score - jnp.max(score, axis=1, keepdims=True))
        total = jnp.sum(weight, axis=1, keepdims=True)
        numer = jnp.dot(weight.astype(jnp.bfloat16), values, preferred_element_type=jnp.float32)
        out_ref[:, h * head : (h + 1) * head] = (numer / total).astype(jnp.bfloat16)

    for m in range(1, n):
        stage(m).wait_send()

    @pl.when(c != k)
    def _():
        stage(0).wait_send()

    for m in far:

        @pl.when(c != k ^ m)
        def _():
            relay(m).wait_send()

    for s in range(n):
        block = c ^ s
        for i in range(2 * len(peers) + 1):
            forward(s, block, k, k ^ 1, i).wait_send()
    for s in range(1, n):
        part_copy(s).wait_send()
    for i in (1, 2, 3):
        kv_copy(i).wait_send()
    seg_copy(0).wait_send()

    @pl.when(c < n - 1)
    def _():
        for i in (4, 5, 6, 7):
            kv_copy(i).wait_send()
        seg_copy(1).wait_send()
        seg_copy(2).wait_send()


def local(n, tokens, w_query, key_value_weight, segment):
    half, depth = tokens.shape
    head = key_value_weight.shape[1]
    width = head + w_query.shape[1]
    hbm = pl.BlockSpec(memory_space=pl.ANY)
    vmem = pl.BlockSpec(memory_space=pltpu.VMEM)
    dma = pltpu.SemaphoreType.DMA
    return pl.pallas_call(
        functools.partial(kernel, n, head),
        out_shape=jax.ShapeDtypeStruct((half, w_query.shape[1]), jnp.bfloat16),
        in_specs=[hbm, hbm, hbm, vmem],
        out_specs=vmem,
        scratch_shapes=[
            pltpu.VMEM((n, half, depth), jnp.bfloat16),
            pltpu.VMEM((n, half // n, depth), jnp.bfloat16),
            pltpu.VMEM((depth, width), jnp.bfloat16),
            pltpu.VMEM((n - 1, half, width), jnp.bfloat16),
            pltpu.VMEM((n - 1, half, width), jnp.bfloat16),
            pltpu.VMEM((half, width), jnp.float32),
            pltpu.VMEM((half, width - head), jnp.bfloat16),
            pltpu.VMEM((2, 4, half, head), jnp.bfloat16),
            pltpu.VMEM((4, 8, half), jnp.int32),
            dma((2,)),
            dma((n,)),
            dma((n,)),
            dma((n,)),
            dma((n, n)),
            dma((n, n)),
            dma((n - 1,)),
            dma((n - 1,)),
            dma((8,)),
            dma((2, 4)),
            dma((3,)),
            dma((4,)),
        ],
        compiler_params=pltpu.CompilerParams(
            collective_id=0, has_side_effects=True, vmem_limit_bytes=60 * 2**20
        ),
    )(tokens, w_query, key_value_weight, segment[None, :])


def solution(mesh):
    in_specs = (P(("ctx", "row"), "col"), P("ctx", "col"), P("ctx", "col"), P(("ctx", "row")))
    out_specs = P(("ctx", "row"), "col")
    step = functools.partial(local, mesh.shape["ctx"])
    return jax.shard_map(step, mesh=mesh, in_specs=in_specs, out_specs=out_specs, check_vma=False)
```

```python
import functools
import math

import jax
import jax.numpy as jnp
from jax import lax
from jax.experimental import pallas as pl
from jax.experimental.pallas import tpu as pltpu
from jax.sharding import PartitionSpec as P

MESH = pl.DeviceIdType.MESH


def kernel(
    n, head, tok_hbm, wq_hbm, wkv_hbm, seg_ref, out_ref,
    whole, staged, weights, part, landed, transit, far_own, own, query, window, segs,
    w_sem, a2a_send, stage_recv, relay_send, tok_recv, fwd_send, part_send, part_recv, transit_recv, kv_send, kv_recv, seg_send, seg_recv,
):
    c, r, k = lax.axis_index("ctx"), lax.axis_index("row"), lax.axis_index("col")
    half = tok_hbm.shape[0]
    rows = half // n
    width = weights.shape[1]
    paired = n == 4
    inner = (c == 1) | (c == 2)

    def block_of(s):
        if paired and s >= 2:
            return jnp.where(c < 2, s, 3 - s)
        return c ^ s

    w_copies = [
        pltpu.make_async_copy(wkv_hbm, weights.at[:, pl.ds(0, head)], w_sem.at[0]),
        pltpu.make_async_copy(wq_hbm, weights.at[:, pl.ds(head, width - head)], w_sem.at[1]),
    ]
    for copy in w_copies:
        copy.start()

    barrier = pltpu.get_barrier_semaphore()

    def greet(i, carry):
        c2, k2 = i // n, i % n

        @pl.when(i != c * n + k)
        def _():
            pl.semaphore_signal(barrier, inc=1, device_id=(c2, r, k2), device_id_type=MESH)

        return carry

    lax.fori_loop(0, n * n, greet, 0)
    for dc in (-1, 0, 1):

        @pl.when((c + dc >= 0) & (c + dc < n))
        def _():
            for dk in (0, 1):
                pl.semaphore_signal(barrier, inc=1, device_id=(c + dc, 1 - r, k ^ dk), device_id_type=MESH)

    ends = jnp.where(c == 0, 1, 0) + jnp.where(c == n - 1, 1, 0)
    pl.semaphore_wait(barrier, n * n - 1 + 6 - 2 * ends)

    def piece(block, j):
        return whole.at[block, pl.ds(pl.multiple_of(j * rows, rows), rows)]

    def landing(ref, sem):
        return pltpu.make_async_copy(ref, ref, sem)

    own_plane = c == k

    def token_rows(j):
        return tok_hbm.at[pl.ds(pl.multiple_of(j * rows, rows), rows)]

    def scatter(m, plane):
        j = k ^ m
        return pltpu.make_async_remote_copy(
            src_ref=token_rows(j), dst_ref=piece(c, j), send_sem=a2a_send.at[m], recv_sem=tok_recv.at[c, j],
            device_id=(plane, r, j), device_id_type=MESH,
        )

    def stage(m):
        j = k ^ m
        return pltpu.make_async_remote_copy(
            src_ref=token_rows(j), dst_ref=staged.at[m], send_sem=a2a_send.at[m], recv_sem=stage_recv.at[m],
            device_id=(c, r, j), device_id_type=MESH,
        )

    def relay(m):
        return pltpu.make_async_remote_copy(
            src_ref=staged.at[m], dst_ref=piece(c, k), send_sem=relay_send.at[m], recv_sem=tok_recv.at[c, k],
            device_id=(k ^ m, r, k), device_id_type=MESH,
        )

    far = list(range(2, n))

    @pl.when(own_plane)
    def _():
        for m in far:
            scatter(m, c).start()
        pltpu.make_async_copy(token_rows(k), piece(c, k), tok_recv.at[c, k]).start()
        scatter(1, c).start()

    @pl.when(c != k)
    def _():
        for m in far:
            stage(m).start()
        for m in (1, 0):
            scatter(m, k).start()

    segs[2 + r] = jnp.broadcast_to(seg_ref[...], segs.shape[1:])

    def seg_copy(i):
        dc, r2 = ((0, 1 - r), (1, r), (1, 1 - r))[i]
        slot = 2 + r if dc == 0 else r
        return pltpu.make_async_remote_copy(
            src_ref=segs.at[2 + r], dst_ref=segs.at[slot], send_sem=seg_send.at[i], recv_sem=seg_recv.at[slot],
            device_id=(c + dc, r2, k), device_id_type=MESH,
        )

    seg_copy(0).start()

    @pl.when(c < n - 1)
    def _():
        seg_copy(1).start()
        seg_copy(2).start()

    for m in far:

        @pl.when(c != k ^ m)
        def _():
            landing(staged.at[m], stage_recv.at[m]).wait()
            relay(m).start()

    def forward(s, block, j, to, index):
        return pltpu.make_async_remote_copy(
            src_ref=piece(block, j), dst_ref=piece(block, j),
            send_sem=fwd_send.at[s, index], recv_sem=tok_recv.at[block, j],
            device_id=(c, r, to), device_id_type=MESH,
        )

    peers = list(range(2, n, 2))

    def step_a(s):
        block = block_of(s)
        landing(piece(block, k), tok_recv.at[block, k]).wait()
        for i, m in enumerate(peers):
            forward(s, block, k, k ^ m, i).start()
        forward(s, block, k, k ^ 1, len(peers)).start()

    def step_b(s):
        block = block_of(s)
        for i, m in enumerate(peers):
            landing(piece(block, k ^ m), tok_recv.at[block, k ^ m]).wait()
            forward(s, block, k ^ m, k ^ 1, len(peers) + 1 + i).start()

    chunk = half // 2

    def part_copy(s, i):
        lines = pl.ds(i * chunk, chunk)
        slot = 1 if paired and s >= 2 else s - 1
        return pltpu.make_async_remote_copy(
            src_ref=part.at[s - 1, lines], dst_ref=landed.at[slot, lines],
            send_sem=part_send.at[s - 1, i], recv_sem=part_recv.at[slot, i],
            device_id=(block_of(s), r, k), device_id_type=MESH,
        )

    def hand_over(s, i):
        lines = pl.ds(i * chunk, chunk)
        return pltpu.make_async_remote_copy(
            src_ref=part.at[s - 1, lines], dst_ref=transit.at[s - 2, lines],
            send_sem=part_send.at[s - 1, i], recv_sem=transit_recv.at[s - 2, i],
            device_id=(c ^ 1, r, k), device_id_type=MESH,
        )

    spans = [(0, head)] + [(lo, min(256, width - lo)) for lo in range(head, width, 256)]

    def step_c(s):
        block = block_of(s)
        for m in [0] + peers:
            landing(piece(block, k ^ 1 ^ m), tok_recv.at[block, k ^ 1 ^ m]).wait()
        if s == 0:
            for copy in w_copies:
                copy.wait()
        for lo, size in spans:
            product = jnp.dot(whole[block], weights[:, lo : lo + size], preferred_element_type=jnp.float32)
            if s == 0:
                own[:, lo : lo + size] = product
            else:
                part[s - 1, :, lo : lo + size] = product.astype(jnp.bfloat16)
                if paired and s >= 2:
                    far_own[s - 2, :, lo : lo + size] = product
        if paired and s >= 2:

            @pl.when(jnp.logical_not(inner))
            def _():
                for i in (0, 1):
                    hand_over(s, i).start()

        elif s:
            for i in (0, 1):
                part_copy(s, i).start()

    def combine(s):
        @pl.when(inner)
        def _():
            for i in (0, 1):
                lines = pl.ds(i * chunk, chunk)
                landing(transit.at[s - 2, lines], transit_recv.at[s - 2, i]).wait()
                total = far_own[s - 2, lines] + transit[s - 2, lines].astype(jnp.float32)
                part[s - 1, lines] = total.astype(jnp.bfloat16)
                part_copy(s, i).start()

    for t in range(n + 2):
        if t < n:
            step_a(t)
        if 0 <= t - 1 < n:
            step_b(t - 1)
        if 0 <= t - 2 < n:
            step_c(t - 2)

    if paired:
        combine(2)
        combine(3)

    slots = landed.shape[0]
    for slot in range(slots):
        for i in (0, 1):
            landing(landed.at[slot, pl.ds(i * chunk, chunk)], part_recv.at[slot, i]).wait()

    def summed(lo, size):
        total = own[:, lo : lo + size]
        for slot in range(slots):
            total = total + landed[slot, :, lo : lo + size].astype(jnp.float32)
        return total.astype(jnp.bfloat16)

    kind = k % 2
    window[kind, 2 + r] = summed(0, head)

    def kv_copy(i):
        dc, dr, dk = i // 4, (i // 2) % 2, i % 2
        r2 = 1 - r if dr else r
        slot = 2 + r if dc == 0 else r
        return pltpu.make_async_remote_copy(
            src_ref=window.at[kind, 2 + r], dst_ref=window.at[kind, slot],
            send_sem=kv_send.at[i], recv_sem=kv_recv.at[kind, slot],
            device_id=(c + dc, r2, k ^ dk), device_id_type=MESH,
        )

    @pl.when(c < n - 1)
    def _():
        for i in (6, 7, 4, 5):
            kv_copy(i).start()

    for i in (2, 3, 1):
        kv_copy(i).start()

    @pl.when(c == 0)
    def _():
        for slot in (0, 1):
            for which in (0, 1):
                window[which, slot] = jnp.zeros((half, head), jnp.bfloat16)
            segs[slot] = jnp.zeros(segs.shape[1:], jnp.int32)

    query[...] = summed(head, width - head)

    landing(segs.at[3 - r], seg_recv.at[3 - r]).wait()

    @pl.when(c > 0)
    def _():
        for slot in (0, 1):
            landing(segs.at[slot], seg_recv.at[slot]).wait()

    key_seg = jnp.concatenate([segs[i][:1] for i in range(4)], axis=1)
    mine = jnp.transpose(jnp.broadcast_to(seg_ref[...], (128, half)))[:, :1]
    keys_n = 4 * half
    key_pos = lax.broadcasted_iota(jnp.int32, (half, keys_n), 1)
    query_pos = lax.broadcasted_iota(jnp.int32, (half, keys_n), 0) + (2 + r) * half
    first = jnp.where(c == 0, 2 * half, 0)
    allow = (key_pos <= query_pos) & (mine == key_seg) & (key_pos >= first)

    landing(window.at[1 - kind, 2 + r], kv_recv.at[1 - kind, 2 + r]).wait()
    for which in (0, 1):
        landing(window.at[which, 3 - r], kv_recv.at[which, 3 - r]).wait()

    @pl.when(c > 0)
    def _():
        for which in (0, 1):
            for slot in (0, 1):
                landing(window.at[which, slot], kv_recv.at[which, slot]).wait()

    keys = window[0].reshape(keys_n, head)
    values = window[1].reshape(keys_n, head)
    scale = 1.0 / math.sqrt(head)
    for h in range((width - head) // head):
        score = lax.dot_general(
            query[:, h * head : (h + 1) * head], keys, (((1,), (1,)), ((), ())), preferred_element_type=jnp.float32
        )
        score = jnp.where(allow, score * scale, -jnp.inf)
        weight = jnp.exp(score - jnp.max(score, axis=1, keepdims=True))
        total = jnp.sum(weight, axis=1, keepdims=True)
        numer = jnp.dot(weight.astype(jnp.bfloat16), values, preferred_element_type=jnp.float32)
        out_ref[:, h * head : (h + 1) * head] = (numer / total).astype(jnp.bfloat16)

    for m in range(1, n):
        stage(m).wait_send()

    @pl.when(c != k)
    def _():
        stage(0).wait_send()

    for m in far:

        @pl.when(c != k ^ m)
        def _():
            relay(m).wait_send()

    for s in range(n):
        block = block_of(s)
        for i in range(2 * len(peers) + 1):
            forward(s, block, k, k ^ 1, i).wait_send()
    for s in range(1, n):
        for i in (0, 1):
            part_copy(s, i).wait_send()
    for i in (1, 2, 3):
        kv_copy(i).wait_send()
    seg_copy(0).wait_send()

    @pl.when(c < n - 1)
    def _():
        for i in (4, 5, 6, 7):
            kv_copy(i).wait_send()
        seg_copy(1).wait_send()
        seg_copy(2).wait_send()


def local(n, tokens, w_query, key_value_weight, segment):
    half, depth = tokens.shape
    head = key_value_weight.shape[1]
    width = head + w_query.shape[1]
    hbm = pl.BlockSpec(memory_space=pl.ANY)
    vmem = pl.BlockSpec(memory_space=pltpu.VMEM)
    dma = pltpu.SemaphoreType.DMA
    return pl.pallas_call(
        functools.partial(kernel, n, head),
        out_shape=jax.ShapeDtypeStruct((half, w_query.shape[1]), jnp.bfloat16),
        in_specs=[hbm, hbm, hbm, vmem],
        out_specs=vmem,
        scratch_shapes=[
            pltpu.VMEM((n, half, depth), jnp.bfloat16),
            pltpu.VMEM((n, half // n, depth), jnp.bfloat16),
            pltpu.VMEM((depth, width), jnp.bfloat16),
            pltpu.VMEM((n - 1, half, width), jnp.bfloat16),
            pltpu.VMEM((2 if n == 4 else n - 1, half, width), jnp.bfloat16),
            pltpu.VMEM((2, half, width), jnp.bfloat16),
            pltpu.VMEM((2, half, width), jnp.float32),
            pltpu.VMEM((half, width), jnp.float32),
            pltpu.VMEM((half, width - head), jnp.bfloat16),
            pltpu.VMEM((2, 4, half, head), jnp.bfloat16),
            pltpu.VMEM((4, 8, half), jnp.int32),
            dma((2,)),
            dma((n,)),
            dma((n,)),
            dma((n,)),
            dma((n, n)),
            dma((n, n)),
            dma((n - 1, 2)),
            dma((n - 1, 2)),
            dma((2, 2)),
            dma((8,)),
            dma((2, 4)),
            dma((3,)),
            dma((4,)),
        ],
        compiler_params=pltpu.CompilerParams(
            collective_id=0, has_side_effects=True, vmem_limit_bytes=60 * 2**20
        ),
    )(tokens, w_query, key_value_weight, segment[None, :])


def solution(mesh):
    in_specs = (P(("ctx", "row"), "col"), P("ctx", "col"), P("ctx", "col"), P(("ctx", "row")))
    out_specs = P(("ctx", "row"), "col")
    step = functools.partial(local, mesh.shape["ctx"])
    return jax.shard_map(step, mesh=mesh, in_specs=in_specs, out_specs=out_specs, check_vma=False)
```

```python
import functools
import math

import jax
import jax.numpy as jnp
from jax import lax
from jax.experimental import pallas as pl
from jax.experimental.pallas import tpu as pltpu
from jax.sharding import PartitionSpec as P

MESH = pl.DeviceIdType.MESH


def kernel(
    n, head, tok_hbm, wq_hbm, wkv_hbm, seg_ref, out_ref,
    whole, staged, weights, part, landed, transit, acc, query, window, segs,
    w_sem, a2a_send, stage_recv, relay_send, tok_recv, fwd_send, part_send, part_recv, transit_recv, kv_send, kv_recv, seg_send, seg_recv,
):
    c, r, k = lax.axis_index("ctx"), lax.axis_index("row"), lax.axis_index("col")
    half = tok_hbm.shape[0]
    rows = half // n
    width = weights.shape[1]
    paired = n == 4
    parts = acc.shape[0] // n
    span = tok_hbm.shape[1] // parts
    own = acc.at[n * (parts - 1)]
    inner = (c == 1) | (c == 2)

    def block_of(s):
        if paired and s >= 2:
            return jnp.where(c < 2, s, 3 - s)
        return c ^ s

    w_copies = [
        pltpu.make_async_copy(wkv_hbm, weights.at[:, pl.ds(0, head)], w_sem.at[0]),
        pltpu.make_async_copy(wq_hbm, weights.at[:, pl.ds(head, width - head)], w_sem.at[1]),
    ]
    for copy in w_copies:
        copy.start()

    barrier = pltpu.get_barrier_semaphore()

    def greet(i, carry):
        c2, k2 = i // n, i % n

        @pl.when(i != c * n + k)
        def _():
            pl.semaphore_signal(barrier, inc=1, device_id=(c2, r, k2), device_id_type=MESH)

        return carry

    lax.fori_loop(0, n * n, greet, 0)
    for dc in (-1, 0, 1):

        @pl.when((c + dc >= 0) & (c + dc < n))
        def _():
            for dk in (0, 1):
                pl.semaphore_signal(barrier, inc=1, device_id=(c + dc, 1 - r, k ^ dk), device_id_type=MESH)

    ends = jnp.where(c == 0, 1, 0) + jnp.where(c == n - 1, 1, 0)
    pl.semaphore_wait(barrier, n * n - 1 + 6 - 2 * ends)

    def piece(block, j, f):
        return whole.at[block, pl.ds(pl.multiple_of(j * rows, rows), rows), pl.ds(f * span, span)]

    def landing(ref, sem):
        return pltpu.make_async_copy(ref, ref, sem)

    own_plane = c == k

    def token_rows(j, f):
        return tok_hbm.at[pl.ds(pl.multiple_of(j * rows, rows), rows), pl.ds(f * span, span)]

    def scatter(m, plane, f):
        j = k ^ m
        return pltpu.make_async_remote_copy(
            src_ref=token_rows(j, f), dst_ref=piece(c, j, f), send_sem=a2a_send.at[f, m], recv_sem=tok_recv.at[f, c, j],
            device_id=(plane, r, j), device_id_type=MESH,
        )

    def stage(m, f):
        j = k ^ m
        return pltpu.make_async_remote_copy(
            src_ref=token_rows(j, f), dst_ref=staged.at[f, m], send_sem=a2a_send.at[f, m], recv_sem=stage_recv.at[f, m],
            device_id=(c, r, j), device_id_type=MESH,
        )

    def relay(m, f):
        return pltpu.make_async_remote_copy(
            src_ref=staged.at[f, m], dst_ref=piece(c, k, f), send_sem=relay_send.at[f, m], recv_sem=tok_recv.at[f, c, k],
            device_id=(k ^ m, r, k), device_id_type=MESH,
        )

    far = list(range(2, n))

    @pl.when(own_plane)
    def _():
        for f in range(parts):
            for m in far:
                scatter(m, c, f).start()
            pltpu.make_async_copy(token_rows(k, f), piece(c, k, f), tok_recv.at[f, c, k]).start()
            scatter(1, c, f).start()

    @pl.when(c != k)
    def _():
        for f in range(parts):
            for m in far:
                stage(m, f).start()
            for m in (1, 0):
                scatter(m, k, f).start()

    segs[2 + r] = jnp.broadcast_to(seg_ref[...], segs.shape[1:])

    def seg_copy(i):
        dc, r2 = ((0, 1 - r), (1, r), (1, 1 - r))[i]
        slot = 2 + r if dc == 0 else r
        return pltpu.make_async_remote_copy(
            src_ref=segs.at[2 + r], dst_ref=segs.at[slot], send_sem=seg_send.at[i], recv_sem=seg_recv.at[slot],
            device_id=(c + dc, r2, k), device_id_type=MESH,
        )

    seg_copy(0).start()

    @pl.when(c < n - 1)
    def _():
        seg_copy(1).start()
        seg_copy(2).start()

    def relays(f):
        for m in far:

            @pl.when(c != k ^ m)
            def _():
                landing(staged.at[f, m], stage_recv.at[f, m]).wait()
                relay(m, f).start()

    relays(0)

    def forward(f, s, block, j, to, index):
        return pltpu.make_async_remote_copy(
            src_ref=piece(block, j, f), dst_ref=piece(block, j, f),
            send_sem=fwd_send.at[f, s, index], recv_sem=tok_recv.at[f, block, j],
            device_id=(c, r, to), device_id_type=MESH,
        )

    peers = list(range(2, n, 2))

    def step_a(f, s):
        block = block_of(s)
        landing(piece(block, k, f), tok_recv.at[f, block, k]).wait()
        for i, m in enumerate(peers):
            forward(f, s, block, k, k ^ m, i).start()
        forward(f, s, block, k, k ^ 1, len(peers)).start()

    def step_b(f, s):
        block = block_of(s)
        for i, m in enumerate(peers):
            landing(piece(block, k ^ m, f), tok_recv.at[f, block, k ^ m]).wait()
            forward(f, s, block, k ^ m, k ^ 1, len(peers) + 1 + i).start()

    chunk = half // 2

    def part_copy(s, i):
        lines = pl.ds(i * chunk, chunk)
        slot = 1 if paired and s >= 2 else s - 1
        return pltpu.make_async_remote_copy(
            src_ref=part.at[s - 1, lines], dst_ref=landed.at[slot, lines],
            send_sem=part_send.at[s - 1, i], recv_sem=part_recv.at[slot, i],
            device_id=(block_of(s), r, k), device_id_type=MESH,
        )

    def hand_over(s, i):
        lines = pl.ds(i * chunk, chunk)
        return pltpu.make_async_remote_copy(
            src_ref=part.at[s - 1, lines], dst_ref=transit.at[s - 2, lines],
            send_sem=part_send.at[s - 1, i], recv_sem=transit_recv.at[s - 2, i],
            device_id=(c ^ 1, r, k), device_id_type=MESH,
        )

    spans = [(0, head)] + [(lo, min(256, width - lo)) for lo in range(head, width, 256)]

    def step_c(f, s):
        block = block_of(s)
        for m in [0] + peers:
            landing(piece(block, k ^ 1 ^ m, f), tok_recv.at[f, block, k ^ 1 ^ m]).wait()
        if f == 0 and s == 0:
            for copy in w_copies:
                copy.wait()
        last = f == parts - 1
        for lo, size in spans:
            product = jnp.dot(
                whole[block, :, f * span : (f + 1) * span],
                weights[f * span : (f + 1) * span, lo : lo + size],
                preferred_element_type=jnp.float32,
            )
            if f:
                product = product + acc[(f - 1) * n + s, :, lo : lo + size]
            if not last or s == 0 or (paired and s >= 2):
                acc[f * n + s, :, lo : lo + size] = product
            if last and s:
                part[s - 1, :, lo : lo + size] = product.astype(jnp.bfloat16)
        if not last:
            return
        if paired and s >= 2:

            @pl.when(jnp.logical_not(inner))
            def _():
                for i in (0, 1):
                    hand_over(s, i).start()

        elif s:
            for i in (0, 1):
                part_copy(s, i).start()

    def combine(s):
        @pl.when(inner)
        def _():
            for i in (0, 1):
                lines = pl.ds(i * chunk, chunk)
                landing(transit.at[s - 2, lines], transit_recv.at[s - 2, i]).wait()
                total = acc[n * (parts - 1) + s, lines] + transit[s - 2, lines].astype(jnp.float32)
                part[s - 1, lines] = total.astype(jnp.bfloat16)
                part_copy(s, i).start()

    units = [(f, s) for f in range(parts) for s in range(n)]
    for t in range(len(units) + 2):
        if t == 1:
            for f in range(1, parts):
                relays(f)
        if t < len(units):
            step_a(*units[t])
        if 0 <= t - 1 < len(units):
            step_b(*units[t - 1])
        if 0 <= t - 2 < len(units):
            step_c(*units[t - 2])

    if paired:
        combine(2)
        combine(3)

    slots = landed.shape[0]
    for slot in range(slots):
        for i in (0, 1):
            landing(landed.at[slot, pl.ds(i * chunk, chunk)], part_recv.at[slot, i]).wait()

    def summed(lo, size):
        total = own[:, lo : lo + size]
        for slot in range(slots):
            total = total + landed[slot, :, lo : lo + size].astype(jnp.float32)
        return total.astype(jnp.bfloat16)

    kind = k % 2
    window[kind, 2 + r] = summed(0, head)

    def kv_copy(i):
        dc, dr, dk = i // 4, (i // 2) % 2, i % 2
        r2 = 1 - r if dr else r
        slot = 2 + r if dc == 0 else r
        return pltpu.make_async_remote_copy(
            src_ref=window.at[kind, 2 + r], dst_ref=window.at[kind, slot],
            send_sem=kv_send.at[i], recv_sem=kv_recv.at[kind, slot],
            device_id=(c + dc, r2, k ^ dk), device_id_type=MESH,
        )

    @pl.when(c < n - 1)
    def _():
        for i in (6, 7, 4, 5):
            kv_copy(i).start()

    for i in (2, 3, 1):
        kv_copy(i).start()

    @pl.when(c == 0)
    def _():
        for slot in (0, 1):
            for which in (0, 1):
                window[which, slot] = jnp.zeros((half, head), jnp.bfloat16)
            segs[slot] = jnp.zeros(segs.shape[1:], jnp.int32)

    query[...] = summed(head, width - head)

    landing(segs.at[3 - r], seg_recv.at[3 - r]).wait()

    @pl.when(c > 0)
    def _():
        for slot in (0, 1):
            landing(segs.at[slot], seg_recv.at[slot]).wait()

    key_seg = jnp.concatenate([segs[i][:1] for i in range(4)], axis=1)
    mine = jnp.transpose(jnp.broadcast_to(seg_ref[...], (128, half)))[:, :1]
    keys_n = 4 * half
    key_pos = lax.broadcasted_iota(jnp.int32, (half, keys_n), 1)
    query_pos = lax.broadcasted_iota(jnp.int32, (half, keys_n), 0) + (2 + r) * half
    first = jnp.where(c == 0, 2 * half, 0)
    allow = (key_pos <= query_pos) & (mine == key_seg) & (key_pos >= first)

    landing(window.at[1 - kind, 2 + r], kv_recv.at[1 - kind, 2 + r]).wait()
    for which in (0, 1):
        landing(window.at[which, 3 - r], kv_recv.at[which, 3 - r]).wait()

    @pl.when(c > 0)
    def _():
        for which in (0, 1):
            for slot in (0, 1):
                landing(window.at[which, slot], kv_recv.at[which, slot]).wait()

    keys = window[0].reshape(keys_n, head)
    values = window[1].reshape(keys_n, head)
    scale = 1.0 / math.sqrt(head)
    for h in range((width - head) // head):
        score = lax.dot_general(
            query[:, h * head : (h + 1) * head], keys, (((1,), (1,)), ((), ())), preferred_element_type=jnp.float32
        )
        score = jnp.where(allow, score * scale, -jnp.inf)
        weight = jnp.exp(score - jnp.max(score, axis=1, keepdims=True))
        total = jnp.sum(weight, axis=1, keepdims=True)
        numer = jnp.dot(weight.astype(jnp.bfloat16), values, preferred_element_type=jnp.float32)
        out_ref[:, h * head : (h + 1) * head] = (numer / total).astype(jnp.bfloat16)

    for f in range(parts):
        for m in range(1, n):
            stage(m, f).wait_send()

        @pl.when(c != k)
        def _():
            stage(0, f).wait_send()

        for m in far:

            @pl.when(c != k ^ m)
            def _():
                relay(m, f).wait_send()

        for s in range(n):
            block = block_of(s)
            for i in range(2 * len(peers) + 1):
                forward(f, s, block, k, k ^ 1, i).wait_send()
    for s in range(1, n):
        for i in (0, 1):
            part_copy(s, i).wait_send()
    for i in (1, 2, 3):
        kv_copy(i).wait_send()
    seg_copy(0).wait_send()

    @pl.when(c < n - 1)
    def _():
        for i in (4, 5, 6, 7):
            kv_copy(i).wait_send()
        seg_copy(1).wait_send()
        seg_copy(2).wait_send()


def local(n, tokens, w_query, key_value_weight, segment):
    half, depth = tokens.shape
    head = key_value_weight.shape[1]
    width = head + w_query.shape[1]
    parts = 2 if n == 4 else 1
    hbm = pl.BlockSpec(memory_space=pl.ANY)
    vmem = pl.BlockSpec(memory_space=pltpu.VMEM)
    dma = pltpu.SemaphoreType.DMA
    return pl.pallas_call(
        functools.partial(kernel, n, head),
        out_shape=jax.ShapeDtypeStruct((half, w_query.shape[1]), jnp.bfloat16),
        in_specs=[hbm, hbm, hbm, vmem],
        out_specs=vmem,
        scratch_shapes=[
            pltpu.VMEM((n, half, depth), jnp.bfloat16),
            pltpu.VMEM((parts, n, half // n, depth // parts), jnp.bfloat16),
            pltpu.VMEM((depth, width), jnp.bfloat16),
            pltpu.VMEM((n - 1, half, width), jnp.bfloat16),
            pltpu.VMEM((2 if n == 4 else n - 1, half, width), jnp.bfloat16),
            pltpu.VMEM((2, half, width), jnp.bfloat16),
            pltpu.VMEM((parts * n, half, width), jnp.float32),
            pltpu.VMEM((half, width - head), jnp.bfloat16),
            pltpu.VMEM((2, 4, half, head), jnp.bfloat16),
            pltpu.VMEM((4, 8, half), jnp.int32),
            dma((2,)),
            dma((parts, n)),
            dma((parts, n)),
            dma((parts, n)),
            dma((parts, n, n)),
            dma((parts, n, n)),
            dma((n - 1, 2)),
            dma((n - 1, 2)),
            dma((2, 2)),
            dma((8,)),
            dma((2, 4)),
            dma((3,)),
            dma((4,)),
        ],
        compiler_params=pltpu.CompilerParams(
            collective_id=0, has_side_effects=True, vmem_limit_bytes=60 * 2**20
        ),
    )(tokens, w_query, key_value_weight, segment[None, :])


def solution(mesh):
    in_specs = (P(("ctx", "row"), "col"), P("ctx", "col"), P("ctx", "col"), P(("ctx", "row")))
    out_specs = P(("ctx", "row"), "col")
    step = functools.partial(local, mesh.shape["ctx"])
    return jax.shard_map(step, mesh=mesh, in_specs=in_specs, out_specs=out_specs, check_vma=False)
```

```python
import functools
import math

import jax
import jax.numpy as jnp
from jax import lax
from jax.experimental import pallas as pl
from jax.experimental.pallas import tpu as pltpu
from jax.sharding import PartitionSpec as P

MESH = pl.DeviceIdType.MESH


def kernel(
    n, head, tok_hbm, wq_hbm, wkv_hbm, seg_ref, out_ref,
    whole, staged, weights, part, landed, transit, far_own, own, query, window, segs,
    w_sem, a2a_send, stage_recv, relay_send, tok_recv, fwd_send, part_send, part_recv, transit_recv, kv_send, kv_recv, seg_send, seg_recv,
):
    c, r, k = lax.axis_index("ctx"), lax.axis_index("row"), lax.axis_index("col")
    half = tok_hbm.shape[0]
    rows = half // n
    width = weights.shape[1]
    paired = n == 4
    inner = (c == 1) | (c == 2)

    def block_of(s):
        if paired and s >= 2:
            return jnp.where(c < 2, s, 3 - s)
        return c ^ s

    w_copies = [
        pltpu.make_async_copy(wkv_hbm, weights.at[:, pl.ds(0, head)], w_sem.at[0]),
        pltpu.make_async_copy(wq_hbm, weights.at[:, pl.ds(head, width - head)], w_sem.at[1]),
    ]
    for copy in w_copies:
        copy.start()

    barrier = pltpu.get_barrier_semaphore()

    def greet(i, carry):
        c2, k2 = i // n, i % n

        @pl.when(i != c * n + k)
        def _():
            pl.semaphore_signal(barrier, inc=1, device_id=(c2, r, k2), device_id_type=MESH)

        return carry

    lax.fori_loop(0, n * n, greet, 0)
    for dc in (-1, 0, 1):

        @pl.when((c + dc >= 0) & (c + dc < n))
        def _():
            for dk in (0, 1):
                pl.semaphore_signal(barrier, inc=1, device_id=(c + dc, 1 - r, k ^ dk), device_id_type=MESH)

    ends = jnp.where(c == 0, 1, 0) + jnp.where(c == n - 1, 1, 0)
    pl.semaphore_wait(barrier, n * n - 1 + 6 - 2 * ends)

    def piece(block, j):
        return whole.at[block, pl.ds(pl.multiple_of(j * rows, rows), rows)]

    def landing(ref, sem):
        return pltpu.make_async_copy(ref, ref, sem)

    own_plane = c == k

    def token_rows(j):
        return tok_hbm.at[pl.ds(pl.multiple_of(j * rows, rows), rows)]

    def scatter(m, plane):
        j = k ^ m
        return pltpu.make_async_remote_copy(
            src_ref=token_rows(j), dst_ref=piece(c, j), send_sem=a2a_send.at[m], recv_sem=tok_recv.at[c, j],
            device_id=(plane, r, j), device_id_type=MESH,
        )

    def stage(m):
        j = k ^ m
        return pltpu.make_async_remote_copy(
            src_ref=token_rows(j), dst_ref=staged.at[m], send_sem=a2a_send.at[m], recv_sem=stage_recv.at[m],
            device_id=(c, r, j), device_id_type=MESH,
        )

    def relay(m):
        return pltpu.make_async_remote_copy(
            src_ref=staged.at[m], dst_ref=piece(c, k), send_sem=relay_send.at[m], recv_sem=tok_recv.at[c, k],
            device_id=(k ^ m, r, k), device_id_type=MESH,
        )

    far = list(range(2, n))

    @pl.when(own_plane)
    def _():
        for m in far:
            scatter(m, c).start()
        pltpu.make_async_copy(token_rows(k), piece(c, k), tok_recv.at[c, k]).start()
        scatter(1, c).start()

    @pl.when(c != k)
    def _():
        for m in far:
            stage(m).start()
        for m in (1, 0):
            scatter(m, k).start()

    segs[2 + r] = jnp.broadcast_to(seg_ref[...], segs.shape[1:])

    def seg_copy(i):
        dc, r2 = ((0, 1 - r), (1, r), (1, 1 - r))[i]
        slot = 2 + r if dc == 0 else r
        return pltpu.make_async_remote_copy(
            src_ref=segs.at[2 + r], dst_ref=segs.at[slot], send_sem=seg_send.at[i], recv_sem=seg_recv.at[slot],
            device_id=(c + dc, r2, k), device_id_type=MESH,
        )

    seg_copy(0).start()

    @pl.when(c < n - 1)
    def _():
        seg_copy(1).start()
        seg_copy(2).start()

    for m in far:

        @pl.when(c != k ^ m)
        def _():
            landing(staged.at[m], stage_recv.at[m]).wait()
            relay(m).start()

    def forward(s, block, j, to, index):
        return pltpu.make_async_remote_copy(
            src_ref=piece(block, j), dst_ref=piece(block, j),
            send_sem=fwd_send.at[s, index], recv_sem=tok_recv.at[block, j],
            device_id=(c, r, to), device_id_type=MESH,
        )

    peers = list(range(2, n, 2))

    def step_a(s):
        block = block_of(s)
        landing(piece(block, k), tok_recv.at[block, k]).wait()
        for i, m in enumerate(peers):
            forward(s, block, k, k ^ m, i).start()
        forward(s, block, k, k ^ 1, len(peers)).start()

    def step_b(s):
        block = block_of(s)
        for i, m in enumerate(peers):
            landing(piece(block, k ^ m), tok_recv.at[block, k ^ m]).wait()
            forward(s, block, k ^ m, k ^ 1, len(peers) + 1 + i).start()

    chunk = half // 4

    def part_copy(s, i):
        lines = pl.ds(i * chunk, chunk)
        slot = 1 if paired and s >= 2 else s - 1
        return pltpu.make_async_remote_copy(
            src_ref=part.at[s - 1, lines], dst_ref=landed.at[slot, lines],
            send_sem=part_send.at[s - 1, i], recv_sem=part_recv.at[slot, i],
            device_id=(block_of(s), r, k), device_id_type=MESH,
        )

    def hand_over(s, i):
        lines = pl.ds(i * chunk, chunk)
        return pltpu.make_async_remote_copy(
            src_ref=part.at[s - 1, lines], dst_ref=transit.at[s - 2, lines],
            send_sem=part_send.at[s - 1, i], recv_sem=transit_recv.at[s - 2, i],
            device_id=(c ^ 1, r, k), device_id_type=MESH,
        )

    spans = [(0, head)] + [(lo, min(256, width - lo)) for lo in range(head, width, 256)]

    def step_c(s):
        block = block_of(s)
        for m in [0] + peers:
            landing(piece(block, k ^ 1 ^ m), tok_recv.at[block, k ^ 1 ^ m]).wait()
        if s == 0:
            for copy in w_copies:
                copy.wait()
        for lo, size in spans:
            product = jnp.dot(whole[block], weights[:, lo : lo + size], preferred_element_type=jnp.float32)
            if s == 0:
                own[:, lo : lo + size] = product
            else:
                part[s - 1, :, lo : lo + size] = product.astype(jnp.bfloat16)
                if paired and s >= 2:
                    far_own[s - 2, :, lo : lo + size] = product
        if paired and s >= 2:

            @pl.when(jnp.logical_not(inner))
            def _():
                for i in range(4):
                    hand_over(s, i).start()

        elif s:
            for i in range(4):
                part_copy(s, i).start()

    def combine(s):
        @pl.when(inner)
        def _():
            for i in range(4):
                lines = pl.ds(i * chunk, chunk)
                landing(transit.at[s - 2, lines], transit_recv.at[s - 2, i]).wait()
                total = far_own[s - 2, lines] + transit[s - 2, lines].astype(jnp.float32)
                part[s - 1, lines] = total.astype(jnp.bfloat16)
                part_copy(s, i).start()

    for t in range(n + 2):
        if t < n:
            step_a(t)
        if 0 <= t - 1 < n:
            step_b(t - 1)
        if 0 <= t - 2 < n:
            step_c(t - 2)

    if paired:
        combine(2)
        combine(3)

    slots = landed.shape[0]
    for slot in range(slots):
        for i in range(4):
            landing(landed.at[slot, pl.ds(i * chunk, chunk)], part_recv.at[slot, i]).wait()

    def summed(lo, size):
        total = own[:, lo : lo + size]
        for slot in range(slots):
            total = total + landed[slot, :, lo : lo + size].astype(jnp.float32)
        return total.astype(jnp.bfloat16)

    kind = k % 2
    window[kind, 2 + r] = summed(0, head)

    def kv_copy(i):
        dc, dr, dk = i // 4, (i // 2) % 2, i % 2
        r2 = 1 - r if dr else r
        slot = 2 + r if dc == 0 else r
        return pltpu.make_async_remote_copy(
            src_ref=window.at[kind, 2 + r], dst_ref=window.at[kind, slot],
            send_sem=kv_send.at[i], recv_sem=kv_recv.at[kind, slot],
            device_id=(c + dc, r2, k ^ dk), device_id_type=MESH,
        )

    @pl.when(c < n - 1)
    def _():
        for i in (6, 7, 4, 5):
            kv_copy(i).start()

    for i in (2, 3, 1):
        kv_copy(i).start()

    @pl.when(c == 0)
    def _():
        for slot in (0, 1):
            for which in (0, 1):
                window[which, slot] = jnp.zeros((half, head), jnp.bfloat16)
            segs[slot] = jnp.zeros(segs.shape[1:], jnp.int32)

    query[...] = summed(head, width - head)

    landing(segs.at[3 - r], seg_recv.at[3 - r]).wait()

    @pl.when(c > 0)
    def _():
        for slot in (0, 1):
            landing(segs.at[slot], seg_recv.at[slot]).wait()

    key_seg = jnp.concatenate([segs[i][:1] for i in range(4)], axis=1)
    mine = jnp.transpose(jnp.broadcast_to(seg_ref[...], (128, half)))[:, :1]
    keys_n = 4 * half
    key_pos = lax.broadcasted_iota(jnp.int32, (half, keys_n), 1)
    query_pos = lax.broadcasted_iota(jnp.int32, (half, keys_n), 0) + (2 + r) * half
    first = jnp.where(c == 0, 2 * half, 0)
    allow = (key_pos <= query_pos) & (mine == key_seg) & (key_pos >= first)

    landing(window.at[1 - kind, 2 + r], kv_recv.at[1 - kind, 2 + r]).wait()
    for which in (0, 1):
        landing(window.at[which, 3 - r], kv_recv.at[which, 3 - r]).wait()

    @pl.when(c > 0)
    def _():
        for which in (0, 1):
            for slot in (0, 1):
                landing(window.at[which, slot], kv_recv.at[which, slot]).wait()

    keys = window[0].reshape(keys_n, head)
    values = window[1].reshape(keys_n, head)
    scale = 1.0 / math.sqrt(head)
    for h in range((width - head) // head):
        score = lax.dot_general(
            query[:, h * head : (h + 1) * head], keys, (((1,), (1,)), ((), ())), preferred_element_type=jnp.float32
        )
        score = jnp.where(allow, score * scale, -jnp.inf)
        weight = jnp.exp(score - jnp.max(score, axis=1, keepdims=True))
        total = jnp.sum(weight, axis=1, keepdims=True)
        numer = jnp.dot(weight.astype(jnp.bfloat16), values, preferred_element_type=jnp.float32)
        out_ref[:, h * head : (h + 1) * head] = (numer / total).astype(jnp.bfloat16)

    for m in range(1, n):
        stage(m).wait_send()

    @pl.when(c != k)
    def _():
        stage(0).wait_send()

    for m in far:

        @pl.when(c != k ^ m)
        def _():
            relay(m).wait_send()

    for s in range(n):
        block = block_of(s)
        for i in range(2 * len(peers) + 1):
            forward(s, block, k, k ^ 1, i).wait_send()
    for s in range(1, n):
        for i in range(4):
            part_copy(s, i).wait_send()
    for i in (1, 2, 3):
        kv_copy(i).wait_send()
    seg_copy(0).wait_send()

    @pl.when(c < n - 1)
    def _():
        for i in (4, 5, 6, 7):
            kv_copy(i).wait_send()
        seg_copy(1).wait_send()
        seg_copy(2).wait_send()


def local(n, tokens, w_query, key_value_weight, segment):
    half, depth = tokens.shape
    head = key_value_weight.shape[1]
    width = head + w_query.shape[1]
    hbm = pl.BlockSpec(memory_space=pl.ANY)
    vmem = pl.BlockSpec(memory_space=pltpu.VMEM)
    dma = pltpu.SemaphoreType.DMA
    return pl.pallas_call(
        functools.partial(kernel, n, head),
        out_shape=jax.ShapeDtypeStruct((half, w_query.shape[1]), jnp.bfloat16),
        in_specs=[hbm, hbm, hbm, vmem],
        out_specs=vmem,
        scratch_shapes=[
            pltpu.VMEM((n, half, depth), jnp.bfloat16),
            pltpu.VMEM((n, half // n, depth), jnp.bfloat16),
            pltpu.VMEM((depth, width), jnp.bfloat16),
            pltpu.VMEM((n - 1, half, width), jnp.bfloat16),
            pltpu.VMEM((2 if n == 4 else n - 1, half, width), jnp.bfloat16),
            pltpu.VMEM((2, half, width), jnp.bfloat16),
            pltpu.VMEM((2, half, width), jnp.float32),
            pltpu.VMEM((half, width), jnp.float32),
            pltpu.VMEM((half, width - head), jnp.bfloat16),
            pltpu.VMEM((2, 4, half, head), jnp.bfloat16),
            pltpu.VMEM((4, 8, half), jnp.int32),
            dma((2,)),
            dma((n,)),
            dma((n,)),
            dma((n,)),
            dma((n, n)),
            dma((n, n)),
            dma((n - 1, 4)),
            dma((n - 1, 4)),
            dma((2, 4)),
            dma((8,)),
            dma((2, 4)),
            dma((3,)),
            dma((4,)),
        ],
        compiler_params=pltpu.CompilerParams(
            collective_id=0, has_side_effects=True, vmem_limit_bytes=60 * 2**20
        ),
    )(tokens, w_query, key_value_weight, segment[None, :])


def solution(mesh):
    in_specs = (P(("ctx", "row"), "col"), P("ctx", "col"), P("ctx", "col"), P(("ctx", "row")))
    out_specs = P(("ctx", "row"), "col")
    step = functools.partial(local, mesh.shape["ctx"])
    return jax.shard_map(step, mesh=mesh, in_specs=in_specs, out_specs=out_specs, check_vma=False)
```
